128 devices in a mesh: feat: 4 (over x), dp: 32 (over z, y, core).
Axes of the slice: x: 4, y: 4, z: 4, core: 2. Of those that a mesh axis runs over, the one named last changes fastest.
Arguments:
- gradients: bfloat16 [64, 16777216], P('dp', 'feat'), may hold values from -6 to 6
- sign_seed: int32 [3], replicated, may hold values from 0 to 1073741823
- sample_index: int32 [8192], replicated, may hold values from 0 to 16777215
- target_sketches: bfloat16 [512, 8192], P('dp'), may hold values from -50 to 50
- target_group: int32 [512], replicated, may hold values from 0 to 15, never falling along the last dimension, each value on 1 to 128 neighbouring positions
Outputs:
- scores: float32 [64, 512], P('dp')
- group_scores: float32 [64, 16], P('dp')
The draws below stay inside these ranges and needn't reach their ends.
Inputs may be any that keep to these rules, and one draw needn't show every extreme that they name: target_group never falls along the targets; each of the 16 groups has 1 to 128 targets, one exactly 128.
All inputs are finite; a program needn't handle non-finite values.
Results may differ from the reference program's by a relative error of at most 0.022.
Values may be sent and summed in bfloat16 or wider, within the bound.
A program may use at most 128 MiB of HBM per device.

```python
import math
import jax
import jax.numpy as jnp
import numpy as np
from jax import lax

P_SIZE = 16777216
K = 8192
NT = 512
TASKS = 16
EX = 64
N_FEAT = 4


def draw_target_sketches(key, part):
    key = jax.random.fold_in(key, 11)
    key_main, key_cols = jax.random.split(key, 2)
    column_scale = jnp.exp(jax.random.uniform(key_cols, (K,), jnp.float32) * math.log(10.0))
    values = jnp.clip(jax.random.normal(key_main, (NT, K), jnp.float32), -5.0, 5.0)
    return (values * column_scale[None, :]).astype(jnp.bfloat16)


def plant(drawn, key, low, largest):
    extent = drawn.shape
    spot = [jax.random.randint(jax.random.fold_in(key, axis), (), 0, extent[axis]) for axis in range(len(extent))]
    drawn = drawn.at[tuple(spot)].set(low)
    longest = extent.index(max(extent))
    spot[longest] = (spot[longest] + 1) % extent[longest]
    return drawn.at[tuple(spot)].set(largest)


def levels(key, shape, shards, low, top_value):
    gain, own = 1.0, jax.random.fold_in(key, 6)
    for axis_at, shards_of in shards:
        steps = jnp.exp(jax.random.uniform(jax.random.fold_in(own, axis_at), (shards_of,), jnp.float32, low / len(shards), top_value / len(shards)))
        gain = gain * jnp.repeat(steps, shape[axis_at] // shards_of).reshape([-1 if axis == axis_at else 1 for axis in range(len(shape))])
    return gain


def length_profile(number_of, total, reach, skew):
    weights = [(1 << 20) // math.isqrt(standing ** skew) + 1 for standing in range(2, number_of + 1)]
    rest, given = total - reach - (number_of - 1), [1] * (number_of - 1)
    while rest > 0:
        movable = [i for i in range(number_of - 1) if given[i] < reach]
        whole, remaining = sum([weights[i] for i in movable]), rest
        for i in movable:
            more = min(reach - given[i], max(1, remaining * weights[i] // whole), rest)
            given[i] = given[i] + more
            rest = rest - more
    return np.array([reach] + given)


def uneven(rng, count, total, reach, slope):
    if count == 2:
        one = jax.random.randint(rng, (), max(1, total - reach), min(reach, total - 1) + 1)
        return jnp.stack([one, total - one])
    sizes = jnp.asarray(length_profile(count, total, reach, slope), jnp.int32)
    twos = (count - 1) // 2
    source_of, taker = sizes[1:1 + 2 * twos:2], sizes[2:2 + 2 * twos:2]
    room = jnp.minimum(source_of - 1, reach - taker)
    shifted = jax.random.randint(jax.random.fold_in(rng, 1), (twos,), 0, 1 << 20) % (room + 1)
    sizes = sizes.at[1:1 + 2 * twos:2].set(source_of - shifted).at[2:2 + 2 * twos:2].set(taker + shifted)
    return sizes[jax.random.permutation(jax.random.fold_in(rng, 2), count)]


def gaussian(own_key, extent, scale, reach, cuts=(), held_as=jnp.bfloat16):
    values = scale * jax.random.normal(own_key, extent, jnp.float32)
    if cuts:
        values = values * levels(own_key, extent, cuts, -0.22, 0.18)
    return jnp.clip(values, -reach, reach).astype(held_as)


def setup_inputs(seed: int = 0) -> dict:
    keys = jax.random.split(jax.random.key(seed), 6)
    gradients = gaussian(keys[0], (EX, P_SIZE), 1.0, 6.0, ((0, 32), (1, 4)))
    sign_seed = jax.random.randint(keys[1], (3,), 0, 1073741824).astype(jnp.int32)
    sample_index = plant(jax.random.randint(keys[2], (K,), 0, P_SIZE), jax.random.fold_in(keys[2], 1), 0, P_SIZE - 1).astype(jnp.int32)
    target_sketches = draw_target_sketches(jax.random.fold_in(keys[5], 71), 0)
    target_group = jnp.searchsorted(jnp.cumsum(uneven(keys[4], TASKS, NT, NT // 4, 1)), jnp.arange(NT), side="right").astype(jnp.int32)
    return dict(gradients=gradients, sign_seed=sign_seed, sample_index=sample_index, target_sketches=target_sketches, target_group=target_group)


EPS = 1e-06

def flip_bits(index, seeds):
    value = index * 747796405 + seeds[0]
    value = value ^ value >> 15 & 131071
    value = value * 277803737 + seeds[1]
    value = value ^ value >> 13 & 524287
    value = value * 1103515245 + seeds[2]
    return value >> 20 & 1

def parity_bits(left, right, count):
    total = jnp.zeros_like(left)
    for place in range(count):
        total = total + (left >> place & 1) * (right >> place & 1)
    return total & 1

def hadamard(order):
    rows = jnp.arange(order, dtype=jnp.int32)
    parity = parity_bits(rows[:, None] + 0 * rows[None, :], rows[None, :] + 0 * rows[:, None], max(order.bit_length() - 1, 0))
    return (1 - 2 * parity).astype(jnp.float32)

def reference(gradients, sign_seed, sample_index, target_sketches, target_group):
    local = P_SIZE // N_FEAT
    outer = local // 16384
    index = jnp.arange(P_SIZE, dtype=jnp.int32)
    bits = flip_bits(index, sign_seed)
    h_small = hadamard(128)
    h_outer = hadamard(outer)
    high = (sample_index // local).astype(jnp.int32)
    low = (sample_index % local).astype(jnp.int32)
    feats = jnp.arange(N_FEAT, dtype=jnp.int32)
    weight = (1 - 2 * parity_bits(high[None, :] + 0 * feats[:, None], feats[:, None] + 0 * high[None, :], max(N_FEAT.bit_length() - 1, 0))).astype(jnp.float32)
    scale = 1.0 / math.sqrt(P_SIZE)

    def one_example(row):
        signed = jnp.where(bits == 1, -row, row).reshape(N_FEAT, outer, 128, 128)
        first = jnp.einsum('fabc,dc->fabd', signed.astype(jnp.float32), h_small, precision=lax.Precision.HIGHEST).astype(jnp.bfloat16)
        second = jnp.einsum('fabc,db->fadc', first.astype(jnp.float32), h_small, precision=lax.Precision.HIGHEST).astype(jnp.bfloat16)
        third = jnp.einsum('fabc,da->fdbc', second.astype(jnp.float32), h_outer, precision=lax.Precision.HIGHEST).astype(jnp.bfloat16)
        picked = jnp.take(third.reshape(N_FEAT, local), low, axis=1).astype(jnp.float32)
        return (lax.optimization_barrier(jnp.sum(picked * weight, axis=0)) * scale).astype(jnp.bfloat16)
    sketch = lax.map(one_example, gradients)
    sketch_wide = sketch.astype(jnp.float32)
    target_wide = target_sketches.astype(jnp.float32)
    squares = lax.optimization_barrier(jnp.sum(sketch_wide * sketch_wide, axis=1))
    target_squares = lax.optimization_barrier(jnp.sum(target_wide * target_wide, axis=1))
    dots = jnp.einsum('ek,tk->et', sketch_wide, target_wide, precision=lax.Precision.HIGHEST)
    scores = dots * lax.rsqrt(squares[:, None] + EPS) * lax.rsqrt(target_squares[None, :] + EPS) * math.sqrt(K)
    onehot = (target_group[:, None] == jnp.arange(TASKS, dtype=jnp.int32)[None, :]).astype(jnp.float32)
    counts = lax.optimization_barrier(jnp.sum(onehot, axis=0))
    group_scores = jnp.dot(scores, onehot, precision=lax.Precision.HIGHEST) / counts[None, :]
    return (scores, group_scores)
```

```python
import functools
import math

import jax
import jax.numpy as jnp
from jax import lax
from jax.experimental import pallas as pl
from jax.experimental.pallas import tpu as pltpu
from jax.sharding import PartitionSpec as P

EPS = 1e-06
TASKS = 16
MULS = (747796405, 277803737, 1103515245)
CHUNKS = 16
UNROLL = 4


def wrap(value):
    value &= 0xFFFFFFFF
    return value - (1 << 32) if value >= 1 << 31 else value


def butterflies(vals):
    vals = list(vals)
    half = 1
    while half < len(vals):
        for start in range(0, len(vals), 2 * half):
            for j in range(start, start + half):
                a, b = vals[j], vals[j + half]
                vals[j], vals[j + half] = a + b, a - b
        half *= 2
    return vals


def parity_signs(left, right):
    x = left & right
    x = x ^ (x >> 4)
    x = x ^ (x >> 2)
    x = x ^ (x >> 1)
    return jnp.where((x & 1) == 1, -1.0, 1.0).astype(jnp.float32)


def aligned(value, by):
    return pl.multiple_of(value, by)


def local_kernel(seed_ref, lane_ref, x_hbm, o_ref, xa, xb, sa, sb, y, t, g, h_ref, w_ref, code, idx_v, idx_s, sems, isem):
    feat = lax.axis_index("feat")
    low = lane_ref[...] & 4194303
    idx_v[...] = ((low >> 13) << 7) | (low & 127)
    index_copy = pltpu.make_async_copy(idx_v, idx_s, isem)
    index_copy.start()

    def fetch(n, buf, which):
        return pltpu.make_async_copy(x_hbm.at[pl.ds(n * 32, 32), :, :], buf, sems.at[which])

    fetch(0, xa, 0).start()
    fetch(1, xb, 1).start()
    r = lax.broadcasted_iota(jnp.int32, (256, 256), 0)
    c = lax.broadcasted_iota(jnp.int32, (256, 256), 1)
    h_ref[...] = parity_signs(r, c).astype(jnp.bfloat16)
    r = lax.broadcasted_iota(jnp.int32, (128, 128), 0)
    c = lax.broadcasted_iota(jnp.int32, (128, 128), 1)
    w_ref[...] = jnp.where((r >> 6) == (c & 1), parity_signs(r & 63, c >> 1), 0.0).astype(jnp.bfloat16)
    s0, s1, s2 = seed_ref[0], seed_ref[1], seed_ref[2] * 2048
    rows = lax.broadcasted_iota(jnp.int32, (8, 128), 0)
    cols = lax.broadcasted_iota(jnp.int32, (8, 128), 1)
    base = (rows * 128 + cols + feat * 4194304) * MULS[0] + s0
    upper = lax.shift_right_logical(rows, 1)
    lower = upper + 4

    def sign(n, qg, x_ref, s_ref):
        start = base + (n * 262144 + qg * 1024) * MULS[0]
        for u in range(2):
            vals = []
            for w4 in range(16):
                w = w4 * 2 + u
                v = start + wrap(w * 8192 * MULS[0])
                v = v ^ lax.shift_right_logical(v, 15)
                v = v * MULS[1] + s1
                v = v ^ lax.shift_right_logical(v, 13)
                v = v * wrap(MULS[2] * 2048) + s2
                flips = jnp.where(v < 0, -1.0, 1.0).astype(jnp.float32)
                pairs = [jnp.take_along_axis(flips, at, axis=0) for at in (upper, lower)]
                both = jnp.concatenate(pairs, axis=0).astype(jnp.bfloat16)
                vals.append(x_ref[w, pl.ds(aligned(qg * 16, 16), 16), :] * both)
            vals = butterflies(vals)
            for w4 in range(16):
                s_ref[w4, pl.ds(aligned(qg * 16, 16), 16), u * 128 : (u + 1) * 128] = vals[w4]

    def transform(n, pair, s_ref):
        rhs = s_ref[pl.ds(pair * 2, 2), :, :].reshape(256, 256)
        out = lax.dot_general(
            h_ref[...], rhs, (((1,), (1,)), ((), ())), preferred_element_type=jnp.float32
        ).astype(jnp.bfloat16)
        y[n, pair * 2] = out[:, :128]
        y[n, pair * 2 + 1] = out[:, 128:]

    def stage(n, x_ref, s_write, s_read):
        def body(i, carry):
            if s_read is not None:
                for a in range(UNROLL):
                    transform(n - 1, i * UNROLL + a, s_read)
            if x_ref is not None:
                for a in range(UNROLL):
                    sign(n, i * UNROLL + a, x_ref, s_write)
            return carry

        lax.fori_loop(0, 8 // UNROLL, body, 0)

    fetch(0, xa, 0).wait()
    stage(0, xa, sa, None)
    fetch(2, xa, 0).start()

    def outer(j, carry):
        n = 2 * j + 1
        fetch(n, xb, 1).wait()
        stage(n, xb, sb, sa)
        fetch(n + 2, xb, 1).start()
        fetch(n + 1, xa, 0).wait()
        stage(n + 1, xa, sa, sb)

        @pl.when(j < CHUNKS // 2 - 2)
        def _():
            fetch(n + 3, xa, 0).start()

        return carry

    lax.fori_loop(0, CHUNKS // 2 - 1, outer, 0)
    fetch(CHUNKS - 1, xb, 1).wait()
    stage(CHUNKS - 1, xb, sb, sa)
    stage(CHUNKS, None, None, sb)

    def across(i, carry):
        m = i >> 2
        o = aligned((i & 3) * 64, 64)
        for a in range(4):
            vals = butterflies([y[n, m, pl.ds(o + a * 16, 16), :] for n in range(CHUNKS)])
            for n in range(CHUNKS):
                t[n, pl.ds(aligned(i * 64 + a * 16, 16), 16), :] = vals[n].astype(jnp.float32)
        return carry

    lax.fori_loop(0, 64, across, 0)
    flat = t.reshape(65536, 128)
    index_copy.wait()

    def pick(kb, carry):
        def row(j, inner):
            for a in range(128):
                at = idx_s[kb * 8 + j, a]
                g[pl.ds(j * 128 + a, 1), :] = flat[pl.ds(at, 1), :]
            return inner

        lax.fori_loop(0, 8, row, 0)
        out = lax.dot_general(
            w_ref[...],
            g[...].astype(jnp.bfloat16),
            (((1,), (1,)), ((), ())),
            preferred_element_type=jnp.float32,
        )
        place = lax.broadcasted_iota(jnp.int32, (64, 128), 0)
        for j in range(8):
            picked = lane_ref[pl.ds(kb * 8 + j, 1), :]
            hit = place == ((picked >> 7) & 63)
            common = (picked >> 22) & feat
            scale = jnp.where((((common >> 1) ^ common) & 1) == 1, -1.0 / 4096, 1.0 / 4096)
            for e in range(2):
                third = jnp.sum(
                    jnp.where(hit, out[e * 64 : (e + 1) * 64, j * 128 : (j + 1) * 128], 0.0),
                    axis=0,
                    keepdims=True,
                )
                code[kb >> 1, e, pl.ds((kb & 1) * 8 + j, 1), :] = third * scale
        return carry

    lax.fori_loop(0, 8, pick, 0)
    o_ref[...] = code[...].astype(jnp.bfloat16)


def local_terms(gradients, sign_seed, sample_index):
    x = gradients.reshape(2, 32768, 128).transpose(1, 0, 2).reshape(512, 128, 128)
    vmem = pltpu.VMEM
    return pl.pallas_call(
        local_kernel,
        out_shape=jax.ShapeDtypeStruct((4, 2, 16, 128), jnp.bfloat16),
        in_specs=[
            pl.BlockSpec(memory_space=pltpu.SMEM),
            pl.BlockSpec(memory_space=pltpu.VMEM),
            pl.BlockSpec(memory_space=pl.ANY),
        ],
        out_specs=pl.BlockSpec(memory_space=pltpu.VMEM),
        scratch_shapes=[
            vmem((32, 128, 128), jnp.bfloat16),
            vmem((32, 128, 128), jnp.bfloat16),
            vmem((16, 128, 256), jnp.bfloat16),
            vmem((16, 128, 256), jnp.bfloat16),
            vmem((16, 16, 256, 128), jnp.bfloat16),
            vmem((16, 4096, 128), jnp.float32),
            vmem((1024, 128), jnp.float32),
            vmem((256, 256), jnp.bfloat16),
            vmem((128, 128), jnp.bfloat16),
            vmem((4, 2, 16, 128), jnp.float32),
            vmem((64, 128), jnp.int32),
            pltpu.SMEM((64, 128), jnp.int32),
            pltpu.SemaphoreType.DMA((2,)),
            pltpu.SemaphoreType.DMA,
        ],
        compiler_params=pltpu.CompilerParams(vmem_limit_bytes=61 * 1024 * 1024),
        cost_estimate=pl.CostEstimate(flops=9_000_000_000, bytes_accessed=17_000_000, transcendentals=0),
    )(sign_seed, sample_index.reshape(64, 128), x)


NT_DIMS = (((1,), (1,)), ((), ()))


def score_kernel(term_ref, group_ref, target_hbm, scores_ref, means_ref, tgt, got, lhs, part, sems, tsem):
    feat = lax.axis_index("feat")
    target_copy = pltpu.make_async_copy(target_hbm, tgt, tsem)
    target_copy.start()
    barrier = pltpu.get_barrier_semaphore()
    peers = [lax.rem(feat + d, 4) for d in (1, 2, 3)]
    for peer in peers:
        pl.semaphore_signal(barrier, inc=1, device_id={"feat": peer}, device_id_type=pl.DeviceIdType.MESH)
    pl.semaphore_wait(barrier, 3)

    def to_peer(source, landing, slot, d):
        return pltpu.make_async_remote_copy(
            src_ref=source,
            dst_ref=landing,
            send_sem=sems.at[slot, 0, d],
            recv_sem=sems.at[slot, 1, d],
            device_id={"feat": peers[d]},
            device_id_type=pl.DeviceIdType.MESH,
        )

    terms = [to_peer(term_ref.at[peers[d]], got.at[d], 0, d) for d in range(3)]
    for copy in terms:
        copy.start()
    target_copy.wait()
    squares = []
    for b in range(4):
        total = jnp.zeros((128, 128), jnp.float32)
        for r in range(16):
            wide = tgt[b * 128 : (b + 1) * 128, r * 128 : (r + 1) * 128].astype(jnp.float32)
            total = total + wide * wide
        squares.append(total)
    squares = jnp.concatenate(squares, axis=0)
    ones = jnp.ones((8, 128), jnp.float32)
    target_squares = lax.dot_general(
        ones, squares, NT_DIMS, precision=lax.Precision.HIGHEST, preferred_element_type=jnp.float32
    )
    for copy in terms:
        copy.wait()
    own = term_ref[feat].astype(jnp.float32)
    for d in range(3):
        own = own + got[d].astype(jnp.float32)
    sketch = own.astype(jnp.bfloat16).astype(jnp.float32)
    lhs[...] = jnp.zeros_like(lhs)
    for e in range(2):
        for r in range(16):
            lhs[e : e + 1, r * 128 : (r + 1) * 128] = sketch[e, r : r + 1, :]
    wide = lhs[...]
    own_squares = jnp.sum(wide * wide, axis=1, keepdims=True)
    dots = lax.dot_general(
        wide.astype(jnp.bfloat16), tgt[...], NT_DIMS, preferred_element_type=jnp.float32
    )
    part[feat, 0] = dots
    part[feat, 1] = target_squares
    part[feat, 2] = jnp.broadcast_to(own_squares, (8, 512))
    parts = [to_peer(part.at[feat], part.at[feat], 1, d) for d in range(3)]
    for copy in parts:
        copy.start()
    member = (lax.broadcasted_iota(jnp.int32, (128, 512), 0) == group_ref[...]).astype(jnp.float32)
    for copy in parts:
        copy.wait()
    whole = (part[0] + part[1]) + (part[2] + part[3])
    scores = whole[0] * lax.rsqrt(whole[2] + EPS) * lax.rsqrt(whole[1] + EPS) * math.sqrt(8192)
    at = lax.broadcasted_iota(jnp.int32, (8, 512), 0)
    sums = lax.dot_general(
        jnp.where(at < 2, scores, 1.0),
        member,
        NT_DIMS,
        precision=lax.Precision.HIGHEST,
        preferred_element_type=jnp.float32,
    )
    scores_ref[...] = scores[:2]
    means_ref[...] = sums[:2, :TASKS] / sums[2:3, :TASKS]


def shards(gradients, sign_seed, sample_index, target_sketches, target_group):
    feat = lax.axis_index("feat")
    share = lax.dynamic_slice(target_sketches, (0, feat * 2048), (16, 2048))
    targets = lax.all_gather(share, "dp", axis=0, tiled=True)
    terms = local_terms(gradients, sign_seed, sample_index)
    vmem = pltpu.VMEM
    return pl.pallas_call(
        score_kernel,
        out_shape=(
            jax.ShapeDtypeStruct((2, 512), jnp.float32),
            jax.ShapeDtypeStruct((2, TASKS), jnp.float32),
        ),
        in_specs=[
            pl.BlockSpec(memory_space=pltpu.VMEM),
            pl.BlockSpec(memory_space=pltpu.VMEM),
            pl.BlockSpec(memory_space=pl.ANY),
        ],
        out_specs=(pl.BlockSpec(memory_space=pltpu.VMEM), pl.BlockSpec(memory_space=pltpu.VMEM)),
        scratch_shapes=[
            vmem((512, 2048), jnp.bfloat16),
            vmem((3, 2, 16, 128), jnp.bfloat16),
            vmem((8, 2048), jnp.float32),
            vmem((4, 3, 8, 512), jnp.float32),
            pltpu.SemaphoreType.DMA((2, 2, 3)),
            pltpu.SemaphoreType.DMA,
        ],
        compiler_params=pltpu.CompilerParams(
            collective_id=0, has_side_effects=True, vmem_limit_bytes=32 * 1024 * 1024
        ),
    )(terms, target_group.reshape(1, 512), targets)


def solution(mesh):
    in_specs = (P("dp", "feat"), P(), P(), P("dp", None), P())
    out_specs = (P("dp", None), P("dp", None))
    return jax.shard_map(shards, mesh=mesh, in_specs=in_specs, out_specs=out_specs, check_vma=False)
```

```python
import functools
import math

import jax
import jax.numpy as jnp
from jax import lax
from jax.experimental import pallas as pl
from jax.experimental.pallas import tpu as pltpu
from jax.sharding import PartitionSpec as P

EPS = 1e-06
NT_DIMS = (((1,), (1,)), ((), ()))
MESH = pl.DeviceIdType.MESH
TASKS = 16
MULS = (747796405, 277803737, 1103515245)
CHUNKS = 16
UNROLL = 4


def wrap(value):
    value &= 0xFFFFFFFF
    return value - (1 << 32) if value >= 1 << 31 else value


def butterflies(vals):
    vals = list(vals)
    half = 1
    while half < len(vals):
        for start in range(0, len(vals), 2 * half):
            for j in range(start, start + half):
                a, b = vals[j], vals[j + half]
                vals[j], vals[j + half] = a + b, a - b
        half *= 2
    return vals


def parity_signs(left, right):
    x = left & right
    x = x ^ (x >> 4)
    x = x ^ (x >> 2)
    x = x ^ (x >> 1)
    return jnp.where((x & 1) == 1, -1.0, 1.0).astype(jnp.float32)


def aligned(value, by):
    return pl.multiple_of(value, by)


def whole_kernel(seed_ref, lane_ref, group_ref, target_hbm, x_hbm, scores_ref, means_ref, xa, xb, sa, sb, y, t, g,
                 h_ref, w_ref, code, idx_v, idx_s, term, got, lhs, tgt, part,
                 sems, isem, tsem, send_sems, recv_sems, feat_sems):
    feat = lax.axis_index("feat")
    me = lax.axis_index("dp")
    low = lane_ref[...] & 4194303
    idx_v[...] = ((low >> 13) << 7) | (low & 127)
    index_copy = pltpu.make_async_copy(idx_v, idx_s, isem)
    index_copy.start()

    def fetch(n, buf, which):
        return pltpu.make_async_copy(x_hbm.at[pl.ds(n * 32, 32), :, :], buf, sems.at[which])

    fetch(0, xa, 0).start()
    fetch(1, xb, 1).start()
    share = target_hbm.at[:, pl.ds(aligned(feat * 2048, 2048), 2048)]
    own_targets = pltpu.make_async_copy(share, tgt.at[me], tsem)
    own_targets.start()
    barrier = pltpu.get_barrier_semaphore()
    peers = [lax.rem(feat + d, 4) for d in (1, 2, 3)]
    for peer in peers:
        pl.semaphore_signal(barrier, inc=1, device_id={"feat": peer}, device_id_type=MESH)

    def greet(j, carry):
        pl.semaphore_signal(barrier, inc=1, device_id={"dp": lax.rem(me + j, 32)}, device_id_type=MESH)
        return carry

    lax.fori_loop(1, 32, greet, 0)
    r = lax.broadcasted_iota(jnp.int32, (256, 256), 0)
    c = lax.broadcasted_iota(jnp.int32, (256, 256), 1)
    h_ref[...] = parity_signs(r, c).astype(jnp.bfloat16)
    r = lax.broadcasted_iota(jnp.int32, (128, 128), 0)
    c = lax.broadcasted_iota(jnp.int32, (128, 128), 1)
    w_ref[...] = jnp.where((r >> 6) == (c & 1), parity_signs(r & 63, c >> 1), 0.0).astype(jnp.bfloat16)
    s0, s1, s2 = seed_ref[0], seed_ref[1], seed_ref[2] * 2048
    rows = lax.broadcasted_iota(jnp.int32, (8, 128), 0)
    cols = lax.broadcasted_iota(jnp.int32, (8, 128), 1)
    base = (rows * 128 + cols + feat * 4194304) * MULS[0] + s0
    upper = lax.shift_right_logical(rows, 1)
    lower = upper + 4

    def sign(n, qg, x_ref, s_ref):
        start = base + (n * 262144 + qg * 1024) * MULS[0]
        for u in range(2):
            vals = []
            for w4 in range(16):
                w = w4 * 2 + u
                v = start + wrap(w * 8192 * MULS[0])
                v = v ^ lax.shift_right_logical(v, 15)
                v = v * MULS[1] + s1
                v = v ^ lax.shift_right_logical(v, 13)
                v = v * wrap(MULS[2] * 2048) + s2
                flips = jnp.where(v < 0, -1.0, 1.0).astype(jnp.float32)
                pairs = [jnp.take_along_axis(flips, at, axis=0) for at in (upper, lower)]
                both = jnp.concatenate(pairs, axis=0).astype(jnp.bfloat16)
                vals.append(x_ref[w, pl.ds(aligned(qg * 16, 16), 16), :] * both)
            vals = butterflies(vals)
            for w4 in range(16):
                s_ref[w4, pl.ds(aligned(qg * 16, 16), 16), u * 128 : (u + 1) * 128] = vals[w4]

    def transform(n, pair, s_ref):
        rhs = s_ref[pl.ds(pair * 2, 2), :, :].reshape(256, 256)
        out = lax.dot_general(
            h_ref[...], rhs, (((1,), (1,)), ((), ())), preferred_element_type=jnp.float32
        ).astype(jnp.bfloat16)
        y[n, pair * 2] = out[:, :128]
        y[n, pair * 2 + 1] = out[:, 128:]

    def stage(n, x_ref, s_write, s_read):
        def body(i, carry):
            if s_read is not None:
                for a in range(UNROLL):
                    transform(n - 1, i * UNROLL + a, s_read)
            if x_ref is not None:
                for a in range(UNROLL):
                    sign(n, i * UNROLL + a, x_ref, s_write)
            return carry

        lax.fori_loop(0, 8 // UNROLL, body, 0)

    def targets_to(j):
        return pltpu.make_async_remote_copy(
            src_ref=tgt.at[me],
            dst_ref=tgt.at[me],
            send_sem=send_sems.at[j],
            recv_sem=recv_sems.at[j],
            device_id={"dp": lax.rem(me + j, 32)},
            device_id_type=MESH,
        )

    def send_targets(j, carry):
        targets_to(j).start()
        return carry

    pl.semaphore_wait(barrier, 34)
    own_targets.wait()
    lax.fori_loop(1, 32, send_targets, 0)
    fetch(0, xa, 0).wait()
    stage(0, xa, sa, None)
    fetch(2, xa, 0).start()

    def outer(j, carry):
        n = 2 * j + 1
        fetch(n, xb, 1).wait()
        stage(n, xb, sb, sa)
        fetch(n + 2, xb, 1).start()
        fetch(n + 1, xa, 0).wait()
        stage(n + 1, xa, sa, sb)

        @pl.when(j < CHUNKS // 2 - 2)
        def _():
            fetch(n + 3, xa, 0).start()

        return carry

    lax.fori_loop(0, CHUNKS // 2 - 1, outer, 0)
    fetch(CHUNKS - 1, xb, 1).wait()
    stage(CHUNKS - 1, xb, sb, sa)
    stage(CHUNKS, None, None, sb)

    def across(i, carry):
        m = i >> 2
        o = aligned((i & 3) * 64, 64)
        for a in range(4):
            vals = butterflies([y[n, m, pl.ds(o + a * 16, 16), :] for n in range(CHUNKS)])
            for n in range(CHUNKS):
                t[n, pl.ds(aligned(i * 64 + a * 16, 16), 16), :] = vals[n].astype(jnp.float32)
        return carry

    lax.fori_loop(0, 64, across, 0)
    flat = t.reshape(65536, 128)
    index_copy.wait()

    def pick(kb, carry):
        def row(j, inner):
            for a in range(128):
                at = idx_s[kb * 8 + j, a]
                g[pl.ds(j * 128 + a, 1), :] = flat[pl.ds(at, 1), :]
            return inner

        lax.fori_loop(0, 8, row, 0)
        out = lax.dot_general(
            w_ref[...],
            g[...].astype(jnp.bfloat16),
            (((1,), (1,)), ((), ())),
            preferred_element_type=jnp.float32,
        )
        place = lax.broadcasted_iota(jnp.int32, (64, 128), 0)
        for j in range(8):
            picked = lane_ref[pl.ds(kb * 8 + j, 1), :]
            hit = place == ((picked >> 7) & 63)
            common = (picked >> 22) & feat
            scale = jnp.where((((common >> 1) ^ common) & 1) == 1, -1.0 / 4096, 1.0 / 4096)
            for e in range(2):
                third = jnp.sum(
                    jnp.where(hit, out[e * 64 : (e + 1) * 64, j * 128 : (j + 1) * 128], 0.0),
                    axis=0,
                    keepdims=True,
                )
                code[kb >> 1, e, pl.ds((kb & 1) * 8 + j, 1), :] = third * scale
        return carry

    lax.fori_loop(0, 8, pick, 0)
    term[...] = code[...].astype(jnp.bfloat16)

    def to_peer(source, landing, slot, d):
        return pltpu.make_async_remote_copy(
            src_ref=source,
            dst_ref=landing,
            send_sem=feat_sems.at[slot, 0, d],
            recv_sem=feat_sems.at[slot, 1, d],
            device_id={"feat": peers[d]},
            device_id_type=MESH,
        )

    terms = [to_peer(term.at[peers[d]], got.at[d], 0, d) for d in range(3)]
    for copy in terms:
        copy.start()
    def wait_targets(j, carry):
        targets_to(j).wait()
        return carry

    lax.fori_loop(1, 32, wait_targets, 0)
    squares = []
    for b in range(4):
        total = jnp.zeros((128, 128), jnp.float32)
        for r in range(16):
            wide = tgt[b * 8 : (b + 1) * 8, :, r * 128 : (r + 1) * 128].reshape(128, 128).astype(jnp.float32)
            total = total + wide * wide
        squares.append(total)
    squares = jnp.concatenate(squares, axis=0)
    ones = jnp.ones((8, 128), jnp.float32)
    target_squares = lax.dot_general(
        ones, squares, NT_DIMS, precision=lax.Precision.HIGHEST, preferred_element_type=jnp.float32
    )
    for copy in terms:
        copy.wait()
    own = term[feat].astype(jnp.float32)
    for d in range(3):
        own = own + got[d].astype(jnp.float32)
    sketch = own.astype(jnp.bfloat16).astype(jnp.float32)
    lhs[...] = jnp.zeros_like(lhs)
    for e in range(2):
        for r in range(16):
            lhs[e : e + 1, r * 128 : (r + 1) * 128] = sketch[e, r : r + 1, :]
    wide = lhs[...]
    own_squares = jnp.sum(wide * wide, axis=1, keepdims=True)
    dots = lax.dot_general(
        wide.astype(jnp.bfloat16), tgt[...].reshape(512, 2048), NT_DIMS, preferred_element_type=jnp.float32
    )
    part[feat, 0] = dots
    part[feat, 1] = target_squares
    part[feat, 2] = jnp.broadcast_to(own_squares, (8, 512))
    parts = [to_peer(part.at[feat], part.at[feat], 1, d) for d in range(3)]
    for copy in parts:
        copy.start()
    member = (lax.broadcasted_iota(jnp.int32, (128, 512), 0) == group_ref[...]).astype(jnp.float32)
    for copy in parts:
        copy.wait()
    whole = (part[0] + part[1]) + (part[2] + part[3])
    scores = whole[0] * lax.rsqrt(whole[2] + EPS) * lax.rsqrt(whole[1] + EPS) * math.sqrt(8192)
    at = lax.broadcasted_iota(jnp.int32, (8, 512), 0)
    sums = lax.dot_general(
        jnp.where(at < 2, scores, 1.0),
        member,
        NT_DIMS,
        precision=lax.Precision.HIGHEST,
        preferred_element_type=jnp.float32,
    )
    scores_ref[...] = scores[:2]
    means_ref[...] = sums[:2, :TASKS] / sums[2:3, :TASKS]


def shards(gradients, sign_seed, sample_index, target_sketches, target_group):
    x = gradients.reshape(2, 32768, 128).transpose(1, 0, 2).reshape(512, 128, 128)
    vmem = pltpu.VMEM
    whole = pl.BlockSpec(memory_space=pltpu.VMEM)
    return pl.pallas_call(
        whole_kernel,
        out_shape=(
            jax.ShapeDtypeStruct((2, 512), jnp.float32),
            jax.ShapeDtypeStruct((2, TASKS), jnp.float32),
        ),
        in_specs=[
            pl.BlockSpec(memory_space=pltpu.SMEM),
            whole,
            whole,
            pl.BlockSpec(memory_space=pl.ANY),
            pl.BlockSpec(memory_space=pl.ANY),
        ],
        out_specs=(whole, whole),
        scratch_shapes=[
            vmem((32, 128, 128), jnp.bfloat16),
            vmem((32, 128, 128), jnp.bfloat16),
            vmem((16, 128, 256), jnp.bfloat16),
            vmem((16, 128, 256), jnp.bfloat16),
            vmem((16, 16, 256, 128), jnp.bfloat16),
            vmem((16, 4096, 128), jnp.float32),
            vmem((1024, 128), jnp.float32),
            vmem((256, 256), jnp.bfloat16),
            vmem((128, 128), jnp.bfloat16),
            vmem((4, 2, 16, 128), jnp.float32),
            vmem((64, 128), jnp.int32),
            pltpu.SMEM((64, 128), jnp.int32),
            vmem((4, 2, 16, 128), jnp.bfloat16),
            vmem((3, 2, 16, 128), jnp.bfloat16),
            vmem((8, 2048), jnp.float32),
            vmem((32, 16, 2048), jnp.bfloat16),
            vmem((4, 3, 8, 512), jnp.float32),
            pltpu.SemaphoreType.DMA((2,)),
            pltpu.SemaphoreType.DMA,
            pltpu.SemaphoreType.DMA,
            pltpu.SemaphoreType.DMA((32,)),
            pltpu.SemaphoreType.DMA((32,)),
            pltpu.SemaphoreType.DMA((2, 2, 3)),
        ],
        compiler_params=pltpu.CompilerParams(
            collective_id=0, has_side_effects=True, vmem_limit_bytes=62 * 1024 * 1024
        ),
    )(sign_seed, sample_index.reshape(64, 128), target_group.reshape(1, 512), target_sketches, x)


def solution(mesh):
    in_specs = (P("dp", "feat"), P(), P(), P("dp", None), P())
    out_specs = (P("dp", None), P("dp", None))
    return jax.shard_map(shards, mesh=mesh, in_specs=in_specs, out_specs=out_specs, check_vma=False)
```

```python
import functools
import math

import jax
import jax.numpy as jnp
from jax import lax
from jax.experimental import pallas as pl
from jax.experimental.pallas import tpu as pltpu
from jax.sharding import PartitionSpec as P

EPS = 1e-06
NT_DIMS = (((1,), (1,)), ((), ()))
MESH = pl.DeviceIdType.MESH
TASKS = 16
MULS = (747796405, 277803737, 1103515245)
CHUNKS = 16
UNROLL = 4


def wrap(value):
    value &= 0xFFFFFFFF
    return value - (1 << 32) if value >= 1 << 31 else value


def butterflies(vals):
    vals = list(vals)
    half = 1
    while half < len(vals):
        for start in range(0, len(vals), 2 * half):
            for j in range(start, start + half):
                a, b = vals[j], vals[j + half]
                vals[j], vals[j + half] = a + b, a - b
        half *= 2
    return vals


def parity_signs(left, right):
    x = left & right
    x = x ^ (x >> 4)
    x = x ^ (x >> 2)
    x = x ^ (x >> 1)
    return jnp.where((x & 1) == 1, -1.0, 1.0).astype(jnp.float32)


def aligned(value, by):
    return pl.multiple_of(value, by)


def whole_kernel(
    seed_hbm, lane_hbm, group_hbm, target_hbm, x_hbm,
    scores_ref, means_ref,
    xbuf, sa, sb, y, t, g, h_ref, w_ref, code, seed_ref, lane_ref, group_ref, idx_v, idx_a, idx_b,
    term, got, lhs, tgt, part,
    x_sems, in_sems, idx_sems, send_sems, recv_sems, feat_sems,
):
    feat = lax.axis_index("feat")
    me = lax.axis_index("dp")

    def fetch(n):
        slot = n & 3
        return pltpu.make_async_copy(x_hbm.at[pl.ds(n * 32, 32), :, :], xbuf.at[slot], x_sems.at[slot])

    seed_copy = pltpu.make_async_copy(seed_hbm, seed_ref, in_sems.at[0])
    lane_copy = pltpu.make_async_copy(lane_hbm, lane_ref, in_sems.at[1])
    group_copy = pltpu.make_async_copy(group_hbm, group_ref, in_sems.at[2])
    share = target_hbm.at[:, pl.ds(aligned(feat * 2048, 2048), 2048)]
    own_targets = pltpu.make_async_copy(share, tgt.at[me], in_sems.at[3])
    seed_copy.start()
    for n in range(4):
        fetch(n).start()
    lane_copy.start()
    group_copy.start()
    own_targets.start()
    barrier = pltpu.get_barrier_semaphore()
    peers = [lax.rem(feat + d, 4) for d in (1, 2, 3)]
    for peer in peers:
        pl.semaphore_signal(barrier, inc=1, device_id={"feat": peer}, device_id_type=MESH)

    def greet(j, carry):
        pl.semaphore_signal(barrier, inc=1, device_id={"dp": lax.rem(me + j, 32)}, device_id_type=MESH)
        return carry

    lax.fori_loop(1, 32, greet, 0)
    r = lax.broadcasted_iota(jnp.int32, (256, 256), 0)
    c = lax.broadcasted_iota(jnp.int32, (256, 256), 1)
    h_ref[...] = parity_signs(r, c).astype(jnp.bfloat16)
    r = lax.broadcasted_iota(jnp.int32, (128, 128), 0)
    c = lax.broadcasted_iota(jnp.int32, (128, 128), 1)
    w_ref[...] = jnp.where((r >> 6) == (c & 1), parity_signs(r & 63, c >> 1), 0.0).astype(jnp.bfloat16)
    seed_copy.wait()
    s0, s1, s2 = seed_ref[0], seed_ref[1], seed_ref[2] * 2048
    rows = lax.broadcasted_iota(jnp.int32, (8, 128), 0)
    cols = lax.broadcasted_iota(jnp.int32, (8, 128), 1)
    base = (rows * 128 + cols + feat * 4194304) * MULS[0] + s0
    upper = lax.shift_right_logical(rows, 1)
    lower = upper + 4

    def sign(n, qg, x_ref, s_ref):
        start = base + (n * 262144 + qg * 1024) * MULS[0]
        for u in range(2):
            vals = []
            for w4 in range(16):
                w = w4 * 2 + u
                v = start + wrap(w * 8192 * MULS[0])
                v = v ^ lax.shift_right_logical(v, 15)
                v = v * MULS[1] + s1
                v = v ^ lax.shift_right_logical(v, 13)
                v = v * wrap(MULS[2] * 2048) + s2
                flips = jnp.where(v < 0, -1.0, 1.0).astype(jnp.float32)
                pairs = [jnp.take_along_axis(flips, at, axis=0) for at in (upper, lower)]
                both = jnp.concatenate(pairs, axis=0).astype(jnp.bfloat16)
                vals.append(x_ref[w, pl.ds(aligned(qg * 16, 16), 16), :] * both)
            vals = butterflies(vals)
            for w4 in range(16):
                s_ref[w4, pl.ds(aligned(qg * 16, 16), 16), u * 128 : (u + 1) * 128] = vals[w4]

    def transform(n, pair, s_ref):
        rhs = s_ref[pl.ds(pair * 2, 2), :, :].reshape(256, 256)
        out = lax.dot_general(
            h_ref[...], rhs, (((1,), (1,)), ((), ())), preferred_element_type=jnp.float32
        ).astype(jnp.bfloat16)
        y[n, pair * 2] = out[:, :128]
        y[n, pair * 2 + 1] = out[:, 128:]

    def stage(n, s_write, s_read, signs=True):
        def body(i, carry):
            if s_read is not None:
                for a in range(UNROLL):
                    transform(n - 1, i * UNROLL + a, s_read)
            if signs:
                for a in range(UNROLL):
                    sign(n, i * UNROLL + a, xbuf.at[n & 3], s_write)
            return carry

        lax.fori_loop(0, 8 // UNROLL, body, 0)

    def targets_to(j):
        return pltpu.make_async_remote_copy(
            src_ref=tgt.at[me],
            dst_ref=tgt.at[me],
            send_sem=send_sems.at[j],
            recv_sem=recv_sems.at[j],
            device_id={"dp": lax.rem(me + j, 32)},
            device_id_type=MESH,
        )

    def send_targets(j, carry):
        targets_to(j).start()
        return carry

    fetch(0).wait()
    stage(0, sa, None)
    fetch(4).start()
    pl.semaphore_wait(barrier, 34)
    own_targets.wait()
    lax.fori_loop(1, 32, send_targets, 0)
    lane_copy.wait()
    low = lane_ref[...] & 4194303
    idx_v[...] = ((low >> 13) << 7) | (low & 127)

    def outer(j, carry):
        n = 2 * j + 1
        fetch(n).wait()
        stage(n, sb, sa)

        @pl.when(j < CHUNKS // 2 - 2)
        def _():
            fetch(n + 4).start()

        fetch(n + 1).wait()
        stage(n + 1, sa, sb)

        @pl.when(j < CHUNKS // 2 - 3)
        def _():
            fetch(n + 5).start()

        return carry

    lax.fori_loop(0, CHUNKS // 2 - 1, outer, 0)
    fetch(CHUNKS - 1).wait()
    stage(CHUNKS - 1, sb, sa)
    stage(CHUNKS, None, sb, signs=False)

    def indices(kb, idx_s, which):
        return pltpu.make_async_copy(idx_v.at[pl.ds(aligned(kb * 8, 8), 8), :], idx_s, idx_sems.at[which])

    indices(0, idx_a, 0).start()
    indices(1, idx_b, 1).start()

    def across(i, carry):
        m = i >> 2
        o = aligned((i & 3) * 64, 64)
        for a in range(4):
            vals = butterflies([y[n, m, pl.ds(o + a * 16, 16), :] for n in range(CHUNKS)])
            for n in range(CHUNKS):
                t[n, pl.ds(aligned(i * 64 + a * 16, 16), 16), :] = vals[n].astype(jnp.float32)
        return carry

    lax.fori_loop(0, 64, across, 0)
    flat = t.reshape(65536, 128)

    def pick(i, half, idx_s):
        kb = 2 * i + half
        indices(kb, idx_s, half).wait()
        for j in range(8):
            for a in range(128):
                at = idx_s[j, a]
                g[j * 128 + a : j * 128 + a + 1, :] = flat[pl.ds(at, 1), :]

        @pl.when(i < 3)
        def _():
            indices(kb + 2, idx_s, half).start()

        out = lax.dot_general(
            w_ref[...], g[...].astype(jnp.bfloat16), NT_DIMS, preferred_element_type=jnp.float32
        )
        place = lax.broadcasted_iota(jnp.int32, (64, 128), 0)
        for j in range(8):
            picked = lane_ref[pl.ds(kb * 8 + j, 1), :]
            hit = place == ((picked >> 7) & 63)
            common = (picked >> 22) & feat
            scale = jnp.where((((common >> 1) ^ common) & 1) == 1, -1.0 / 4096, 1.0 / 4096)
            for e in range(2):
                mine = jnp.where(hit, out[e * 64 : (e + 1) * 64, j * 128 : (j + 1) * 128], 0.0)
                third = jnp.sum(mine, axis=0, keepdims=True)
                row = half * 8 + j
                code[i, e, row : row + 1, :] = third * scale

    def pick_two(i, carry):
        pick(i, 0, idx_a)
        pick(i, 1, idx_b)
        return carry

    lax.fori_loop(0, 4, pick_two, 0)
    term[...] = code[...].astype(jnp.bfloat16)

    def to_peer(source, landing, slot, d):
        return pltpu.make_async_remote_copy(
            src_ref=source,
            dst_ref=landing,
            send_sem=feat_sems.at[slot, 0, d],
            recv_sem=feat_sems.at[slot, 1, d],
            device_id={"feat": peers[d]},
            device_id_type=MESH,
        )

    terms = [to_peer(term.at[peers[d]], got.at[d], 0, d) for d in range(3)]
    for copy in terms:
        copy.start()
    def wait_targets(j, carry):
        targets_to(j).wait()
        return carry

    lax.fori_loop(1, 32, wait_targets, 0)
    squares = []
    for b in range(4):
        total = jnp.zeros((128, 128), jnp.float32)
        for r in range(16):
            wide = tgt[b * 8 : (b + 1) * 8, :, r * 128 : (r + 1) * 128].reshape(128, 128).astype(jnp.float32)
            total = total + wide * wide
        squares.append(total)
    squares = jnp.concatenate(squares, axis=0)
    ones = jnp.ones((8, 128), jnp.float32)
    target_squares = lax.dot_general(
        ones, squares, NT_DIMS, precision=lax.Precision.HIGHEST, preferred_element_type=jnp.float32
    )
    for copy in terms:
        copy.wait()
    own = term[feat].astype(jnp.float32)
    for d in range(3):
        own = own + got[d].astype(jnp.float32)
    sketch = own.astype(jnp.bfloat16).astype(jnp.float32)
    lhs[...] = jnp.zeros_like(lhs)
    for e in range(2):
        for r in range(16):
            lhs[e : e + 1, r * 128 : (r + 1) * 128] = sketch[e, r : r + 1, :]
    wide = lhs[...]
    own_squares = jnp.sum(wide * wide, axis=1, keepdims=True)
    dots = lax.dot_general(
        wide.astype(jnp.bfloat16), tgt[...].reshape(512, 2048), NT_DIMS, preferred_element_type=jnp.float32
    )
    part[feat, 0] = dots
    part[feat, 1] = target_squares
    part[feat, 2] = jnp.broadcast_to(own_squares, (8, 512))
    parts = [to_peer(part.at[feat], part.at[feat], 1, d) for d in range(3)]
    for copy in parts:
        copy.start()
    group_copy.wait()
    member = (lax.broadcasted_iota(jnp.int32, (128, 512), 0) == group_ref[...]).astype(jnp.float32)
    member = member.astype(jnp.bfloat16)
    for copy in parts:
        copy.wait()
    whole = (part[0] + part[1]) + (part[2] + part[3])
    scores = whole[0] * lax.rsqrt(whole[2] + EPS) * lax.rsqrt(whole[1] + EPS) * math.sqrt(8192)
    at = lax.broadcasted_iota(jnp.int32, (8, 512), 0)
    rest = scores
    sums = jnp.zeros((8, 128), jnp.float32)
    for piece in range(3):
        top = rest.astype(jnp.bfloat16)
        rest = rest - top.astype(jnp.float32)
        filled = jnp.where(at < 2, top.astype(jnp.float32), 1.0 if piece == 0 else 0.0)
        sums = sums + lax.dot_general(
            filled.astype(jnp.bfloat16), member, NT_DIMS, preferred_element_type=jnp.float32
        )
    scores_ref[...] = scores[:2]
    means_ref[...] = sums[:2, :TASKS] / sums[2:3, :TASKS]


def shards(gradients, sign_seed, sample_index, target_sketches, target_group):
    x = gradients.reshape(2, 32768, 128).transpose(1, 0, 2).reshape(512, 128, 128)
    vmem = pltpu.VMEM
    whole = pl.BlockSpec(memory_space=pltpu.VMEM)
    dma = pltpu.SemaphoreType.DMA
    return pl.pallas_call(
        whole_kernel,
        out_shape=(
            jax.ShapeDtypeStruct((2, 512), jnp.float32),
            jax.ShapeDtypeStruct((2, TASKS), jnp.float32),
        ),
        in_specs=[pl.BlockSpec(memory_space=pl.ANY)] * 5,
        out_specs=(whole, whole),
        scratch_shapes=[
            vmem((4, 32, 128, 128), jnp.bfloat16),
            vmem((16, 128, 256), jnp.bfloat16),
            vmem((16, 128, 256), jnp.bfloat16),
            vmem((16, 16, 256, 128), jnp.bfloat16),
            vmem((16, 4096, 128), jnp.float32),
            vmem((1024, 128), jnp.float32),
            vmem((256, 256), jnp.bfloat16),
            vmem((128, 128), jnp.bfloat16),
            vmem((4, 2, 16, 128), jnp.float32),
            pltpu.SMEM((3,), jnp.int32),
            vmem((64, 128), jnp.int32),
            vmem((1, 512), jnp.int32),
            vmem((64, 128), jnp.int32),
            pltpu.SMEM((8, 128), jnp.int32),
            pltpu.SMEM((8, 128), jnp.int32),
            vmem((4, 2, 16, 128), jnp.bfloat16),
            vmem((3, 2, 16, 128), jnp.bfloat16),
            vmem((8, 2048), jnp.float32),
            vmem((32, 16, 2048), jnp.bfloat16),
            vmem((4, 3, 8, 512), jnp.float32),
            dma((4,)),
            dma((4,)),
            dma((2,)),
            dma((32,)),
            dma((32,)),
            dma((2, 2, 3)),
        ],
        compiler_params=pltpu.CompilerParams(
            collective_id=0, has_side_effects=True, vmem_limit_bytes=60 * 1024 * 1024
        ),
    )(sign_seed, sample_index.reshape(64, 128), target_group.reshape(1, 512), target_sketches, x)


def solution(mesh):
    in_specs = (P("dp", "feat"), P(), P(), P("dp", None), P())
    out_specs = (P("dp", None), P("dp", None))
    return jax.shard_map(shards, mesh=mesh, in_specs=in_specs, out_specs=out_specs, check_vma=False)
```

```python
import functools
import math

import jax
import jax.numpy as jnp
from jax import lax
from jax.experimental import pallas as pl
from jax.experimental.pallas import tpu as pltpu
from jax.sharding import PartitionSpec as P

EPS = 1e-06
NT_DIMS = (((1,), (1,)), ((), ()))
MESH = pl.DeviceIdType.MESH
TASKS = 16
MULS = (747796405, 277803737, 1103515245)
CHUNKS = 16
UNROLL = 4


def wrap(value):
    value &= 0xFFFFFFFF
    return value - (1 << 32) if value >= 1 << 31 else value


def butterflies(vals):
    vals = list(vals)
    half = 1
    while half < len(vals):
        for start in range(0, len(vals), 2 * half):
            for j in range(start, start + half):
                a, b = vals[j], vals[j + half]
                vals[j], vals[j + half] = a + b, a - b
        half *= 2
    return vals


def parity_signs(left, right):
    x = left & right
    x = x ^ (x >> 4)
    x = x ^ (x >> 2)
    x = x ^ (x >> 1)
    return jnp.where((x & 1) == 1, -1.0, 1.0).astype(jnp.float32)


def aligned(value, by):
    return pl.multiple_of(value, by)


def whole_kernel(
    seed_hbm, lane_hbm, group_hbm, target_hbm, x_hbm,
    scores_ref, means_ref,
    xbuf, sa, sb, t, g, h_ref, w_ref, code, seed_ref, lane_ref, group_ref, idx_v, idx_a, idx_b,
    term, got, lhs, tgt, part,
    x_sems, in_sems, idx_sems, send_sems, recv_sems, feat_sems,
):
    feat = lax.axis_index("feat")
    me = lax.axis_index("dp")

    def fetch(n):
        slot = n & 3
        return pltpu.make_async_copy(x_hbm.at[pl.ds(n * 32, 32), :, :], xbuf.at[slot], x_sems.at[slot])

    seed_copy = pltpu.make_async_copy(seed_hbm, seed_ref, in_sems.at[0])
    lane_copy = pltpu.make_async_copy(lane_hbm, lane_ref, in_sems.at[1])
    group_copy = pltpu.make_async_copy(group_hbm, group_ref, in_sems.at[2])
    share = target_hbm.at[:, pl.ds(aligned(feat * 2048, 2048), 2048)]
    own_targets = pltpu.make_async_copy(share, tgt.at[me], in_sems.at[3])
    seed_copy.start()
    for n in range(4):
        fetch(n).start()
    lane_copy.start()
    group_copy.start()
    own_targets.start()
    barrier = pltpu.get_barrier_semaphore()
    peers = [lax.rem(feat + d, 4) for d in (1, 2, 3)]
    for peer in peers:
        pl.semaphore_signal(barrier, inc=1, device_id={"feat": peer}, device_id_type=MESH)

    def greet(j, carry):
        pl.semaphore_signal(barrier, inc=1, device_id={"dp": lax.rem(me + j, 32)}, device_id_type=MESH)
        return carry

    lax.fori_loop(1, 32, greet, 0)
    r = lax.broadcasted_iota(jnp.int32, (256, 256), 0)
    c = lax.broadcasted_iota(jnp.int32, (256, 256), 1)
    h_ref[...] = parity_signs(r, c).astype(jnp.bfloat16)
    r = lax.broadcasted_iota(jnp.int32, (128, 128), 0)
    c = lax.broadcasted_iota(jnp.int32, (128, 128), 1)
    w_ref[...] = jnp.where((r >> 6) == (c & 1), parity_signs(r & 63, c >> 1), 0.0).astype(jnp.bfloat16)
    seed_copy.wait()
    s0, s1, s2 = seed_ref[0], seed_ref[1], seed_ref[2] * 2048
    rows = lax.broadcasted_iota(jnp.int32, (8, 128), 0)
    cols = lax.broadcasted_iota(jnp.int32, (8, 128), 1)
    base = (rows * 128 + cols + feat * 4194304) * MULS[0] + s0
    upper = lax.shift_right_logical(rows, 1)
    lower = upper + 4

    def sign(n, qg, x_ref, s_ref):
        start = base + (n * 262144 + qg * 1024) * MULS[0]
        for u in range(2):
            vals = []
            for w4 in range(16):
                w = w4 * 2 + u
                v = start + wrap(w * 8192 * MULS[0])
                v = v ^ lax.shift_right_logical(v, 15)
                v = v * MULS[1] + s1
                v = v ^ lax.shift_right_logical(v, 13)
                v = v * wrap(MULS[2] * 2048) + s2
                flips = jnp.where(v < 0, -1.0, 1.0).astype(jnp.float32)
                pairs = [jnp.take_along_axis(flips, at, axis=0) for at in (upper, lower)]
                both = jnp.concatenate(pairs, axis=0).astype(jnp.bfloat16)
                vals.append(x_ref[w, pl.ds(aligned(qg * 16, 16), 16), :] * both)
            vals = butterflies(vals)
            for w4 in range(16):
                s_ref[w4, pl.ds(aligned(qg * 16, 16), 16), u * 128 : (u + 1) * 128] = vals[w4]

    def transform(n, pair, s_ref):
        rhs = s_ref[pl.ds(pair * 2, 2), :, :].reshape(256, 256)
        out = lax.dot_general(h_ref[...], rhs, NT_DIMS, preferred_element_type=jnp.float32)
        at = aligned(pair * 512, 512)
        t[n, pl.ds(at, 256), :] = out[:, :128]
        t[n, pl.ds(at + 256, 256), :] = out[:, 128:]

    def stage(n, s_write, s_read, signs=True):
        def body(i, carry):
            for a in range(UNROLL):
                if signs:
                    sign(n, i * UNROLL + a, xbuf.at[n & 3], s_write)
                if s_read is not None:
                    transform(n - 1, i * UNROLL + a, s_read)
            return carry

        lax.fori_loop(0, 8 // UNROLL, body, 0)

    def targets_to(j):
        return pltpu.make_async_remote_copy(
            src_ref=tgt.at[me],
            dst_ref=tgt.at[me],
            send_sem=send_sems.at[j],
            recv_sem=recv_sems.at[j],
            device_id={"dp": lax.rem(me + j, 32)},
            device_id_type=MESH,
        )

    def send_targets(j, carry):
        targets_to(j).start()
        return carry

    fetch(0).wait()
    stage(0, sa, None)
    fetch(4).start()
    pl.semaphore_wait(barrier, 34)
    own_targets.wait()
    lax.fori_loop(1, 32, send_targets, 0)
    lane_copy.wait()
    low = lane_ref[...] & 4194303
    idx_v[...] = ((low >> 13) << 7) | (low & 127)

    def outer(j, carry):
        n = 2 * j + 1
        fetch(n).wait()
        stage(n, sb, sa)

        @pl.when(j < CHUNKS // 2 - 2)
        def _():
            fetch(n + 4).start()

        fetch(n + 1).wait()
        stage(n + 1, sa, sb)

        @pl.when(j < CHUNKS // 2 - 3)
        def _():
            fetch(n + 5).start()

        return carry

    lax.fori_loop(0, CHUNKS // 2 - 1, outer, 0)
    fetch(CHUNKS - 1).wait()
    stage(CHUNKS - 1, sb, sa)
    stage(CHUNKS, None, sb, signs=False)

    def indices(kb, idx_s, which):
        return pltpu.make_async_copy(idx_v.at[pl.ds(aligned(kb * 8, 8), 8), :], idx_s, idx_sems.at[which])

    indices(0, idx_a, 0).start()
    indices(1, idx_b, 1).start()

    def across(i, carry):
        for a in range(16):
            rows8 = pl.ds(aligned(i * 128, 128) + a * 8, 8)
            vals = butterflies([t[n, rows8, :] for n in range(CHUNKS)])
            for n in range(CHUNKS):
                t[n, rows8, :] = vals[n]
        return carry

    lax.fori_loop(0, 32, across, 0)
    flat = t.reshape(65536, 128)

    def pick(i, half, idx_s):
        kb = 2 * i + half
        indices(kb, idx_s, half).wait()
        for j in range(8):
            for a in range(128):
                at = idx_s[j, a]
                g[j * 128 + a : j * 128 + a + 1, :] = flat[pl.ds(at, 1), :]

        @pl.when(i < 3)
        def _():
            indices(kb + 2, idx_s, half).start()

        out = lax.dot_general(
            w_ref[...], g[...].astype(jnp.bfloat16), NT_DIMS, preferred_element_type=jnp.float32
        )
        place = lax.broadcasted_iota(jnp.int32, (64, 128), 0)
        for j in range(8):
            picked = lane_ref[pl.ds(kb * 8 + j, 1), :]
            hit = place == ((picked >> 7) & 63)
            common = (picked >> 22) & feat
            scale = jnp.where((((common >> 1) ^ common) & 1) == 1, -1.0 / 4096, 1.0 / 4096)
            for e in range(2):
                mine = jnp.where(hit, out[e * 64 : (e + 1) * 64, j * 128 : (j + 1) * 128], 0.0)
                third = jnp.sum(mine, axis=0, keepdims=True)
                row = half * 8 + j
                code[i, e, row : row + 1, :] = third * scale

    def pick_two(i, carry):
        pick(i, 0, idx_a)
        pick(i, 1, idx_b)
        return carry

    lax.fori_loop(0, 4, pick_two, 0)
    term[...] = code[...].astype(jnp.bfloat16)

    def to_peer(source, landing, slot, d):
        return pltpu.make_async_remote_copy(
            src_ref=source,
            dst_ref=landing,
            send_sem=feat_sems.at[slot, 0, d],
            recv_sem=feat_sems.at[slot, 1, d],
            device_id={"feat": peers[d]},
            device_id_type=MESH,
        )

    terms = [to_peer(term.at[peers[d]], got.at[d], 0, d) for d in range(3)]
    for copy in terms:
        copy.start()
    def wait_targets(j, carry):
        targets_to(j).wait()
        return carry

    lax.fori_loop(1, 32, wait_targets, 0)
    squares = []
    for b in range(4):
        total = jnp.zeros((128, 128), jnp.float32)
        for r in range(16):
            wide = tgt[b * 8 : (b + 1) * 8, :, r * 128 : (r + 1) * 128].reshape(128, 128).astype(jnp.float32)
            total = total + wide * wide
        squares.append(total)
    squares = jnp.concatenate(squares, axis=0)
    ones = jnp.ones((8, 128), jnp.float32)
    target_squares = lax.dot_general(
        ones, squares, NT_DIMS, precision=lax.Precision.HIGHEST, preferred_element_type=jnp.float32
    )
    for copy in terms:
        copy.wait()
    own = term[feat].astype(jnp.float32)
    for d in range(3):
        own = own + got[d].astype(jnp.float32)
    sketch = own.astype(jnp.bfloat16).astype(jnp.float32)
    lhs[...] = jnp.zeros_like(lhs)
    for e in range(2):
        for r in range(16):
            lhs[e : e + 1, r * 128 : (r + 1) * 128] = sketch[e, r : r + 1, :]
    wide = lhs[...]
    own_squares = jnp.sum(wide * wide, axis=1, keepdims=True)
    dots = lax.dot_general(
        wide.astype(jnp.bfloat16), tgt[...].reshape(512, 2048), NT_DIMS, preferred_element_type=jnp.float32
    )
    part[feat, 0] = dots
    part[feat, 1] = target_squares
    part[feat, 2] = jnp.broadcast_to(own_squares, (8, 512))
    parts = [to_peer(part.at[feat], part.at[feat], 1, d) for d in range(3)]
    for copy in parts:
        copy.start()
    group_copy.wait()
    member = (lax.broadcasted_iota(jnp.int32, (128, 512), 0) == group_ref[...]).astype(jnp.float32)
    member = member.astype(jnp.bfloat16)
    for copy in parts:
        copy.wait()
    whole = (part[0] + part[1]) + (part[2] + part[3])
    scores = whole[0] * lax.rsqrt(whole[2] + EPS) * lax.rsqrt(whole[1] + EPS) * math.sqrt(8192)
    at = lax.broadcasted_iota(jnp.int32, (8, 512), 0)
    rest = scores
    sums = jnp.zeros((8, 128), jnp.float32)
    for piece in range(3):
        top = rest.astype(jnp.bfloat16)
        rest = rest - top.astype(jnp.float32)
        filled = jnp.where(at < 2, top.astype(jnp.float32), 1.0 if piece == 0 else 0.0)
        sums = sums + lax.dot_general(
            filled.astype(jnp.bfloat16), member, NT_DIMS, preferred_element_type=jnp.float32
        )
    scores_ref[...] = scores[:2]
    means_ref[...] = sums[:2, :TASKS] / sums[2:3, :TASKS]


def shards(gradients, sign_seed, sample_index, target_sketches, target_group):
    x = gradients.reshape(2, 32768, 128).transpose(1, 0, 2).reshape(512, 128, 128)
    vmem = pltpu.VMEM
    whole = pl.BlockSpec(memory_space=pltpu.VMEM)
    dma = pltpu.SemaphoreType.DMA
    return pl.pallas_call(
        whole_kernel,
        out_shape=(
            jax.ShapeDtypeStruct((2, 512), jnp.float32),
            jax.ShapeDtypeStruct((2, TASKS), jnp.float32),
        ),
        in_specs=[pl.BlockSpec(memory_space=pltpu.HBM)] * 5,
        out_specs=(whole, whole),
        scratch_shapes=[
            vmem((4, 32, 128, 128), jnp.bfloat16),
            vmem((16, 128, 256), jnp.bfloat16),
            vmem((16, 128, 256), jnp.bfloat16),
            vmem((16, 4096, 128), jnp.float32),
            vmem((1024, 128), jnp.float32),
            vmem((256, 256), jnp.bfloat16),
            vmem((128, 128), jnp.bfloat16),
            vmem((4, 2, 16, 128), jnp.float32),
            pltpu.SMEM((3,), jnp.int32),
            vmem((64, 128), jnp.int32),
            vmem((1, 512), jnp.int32),
            vmem((64, 128), jnp.int32),
            pltpu.SMEM((8, 128), jnp.int32),
            pltpu.SMEM((8, 128), jnp.int32),
            vmem((4, 2, 16, 128), jnp.bfloat16),
            vmem((3, 2, 16, 128), jnp.bfloat16),
            vmem((8, 2048), jnp.float32),
            vmem((32, 16, 2048), jnp.bfloat16),
            vmem((4, 3, 8, 512), jnp.float32),
            dma((4,)),
            dma((4,)),
            dma((2,)),
            dma((32,)),
            dma((32,)),
            dma((2, 2, 3)),
        ],
        compiler_params=pltpu.CompilerParams(
            collective_id=0, has_side_effects=True, vmem_limit_bytes=48 * 1024 * 1024
        ),
    )(sign_seed, sample_index.reshape(64, 128), target_group.reshape(1, 512), target_sketches, x)


def solution(mesh):
    in_specs = (P("dp", "feat"), P(), P(), P("dp", None), P())
    out_specs = (P("dp", None), P("dp", None))
    return jax.shard_map(shards, mesh=mesh, in_specs=in_specs, out_specs=out_specs, check_vma=False)
```

```python
import functools
import math

import jax
import jax.numpy as jnp
from jax import lax
from jax.experimental import pallas as pl
from jax.experimental.pallas import tpu as pltpu
from jax.sharding import PartitionSpec as P

EPS = 1e-06
NT_DIMS = (((1,), (1,)), ((), ()))
MESH = pl.DeviceIdType.MESH
TASKS = 16
MULS = (747796405, 277803737, 1103515245)
CHUNKS = 16
UNROLL = 4


def wrap(value):
    value &= 0xFFFFFFFF
    return value - (1 << 32) if value >= 1 << 31 else value


def butterflies(vals):
    vals = list(vals)
    half = 1
    while half < len(vals):
        for start in range(0, len(vals), 2 * half):
            for j in range(start, start + half):
                a, b = vals[j], vals[j + half]
                vals[j], vals[j + half] = a + b, a - b
        half *= 2
    return vals


def parity_signs(left, right):
    x = left & right
    x = x ^ (x >> 4)
    x = x ^ (x >> 2)
    x = x ^ (x >> 1)
    return jnp.where((x & 1) == 1, -1.0, 1.0).astype(jnp.float32)


def aligned(value, by):
    return pl.multiple_of(value, by)


def whole_kernel(
    seed_hbm, lane_hbm, group_hbm, target_hbm, x_hbm,
    scores_ref, means_ref,
    xbuf, sa, sb, t, ga, gb, h_ref, w_ref, code, seed_ref, lane_ref, group_ref, idx_v, idx_a, idx_b,
    term, got, lhs, tgt, part,
    x_sems, in_sems, idx_sems, send_sems, recv_sems, feat_sems,
):
    feat = lax.axis_index("feat")
    me = lax.axis_index("dp")

    def fetch(n):
        slot = n & 3
        return pltpu.make_async_copy(x_hbm.at[pl.ds(n * 32, 32), :, :], xbuf.at[slot], x_sems.at[slot])

    seed_copy = pltpu.make_async_copy(seed_hbm, seed_ref, in_sems.at[0])
    lane_copy = pltpu.make_async_copy(lane_hbm, lane_ref, in_sems.at[1])
    group_copy = pltpu.make_async_copy(group_hbm, group_ref, in_sems.at[2])
    share = target_hbm.at[:, pl.ds(aligned(feat * 2048, 2048), 2048)]
    own_targets = pltpu.make_async_copy(share, tgt.at[me], in_sems.at[3])
    seed_copy.start()
    for n in range(2):
        fetch(n).start()
    lane_copy.start()
    group_copy.start()
    own_targets.start()
    barrier = pltpu.get_barrier_semaphore()
    peers = [lax.rem(feat + d, 4) for d in (1, 2, 3)]
    for peer in peers:
        pl.semaphore_signal(barrier, inc=1, device_id={"feat": peer}, device_id_type=MESH)

    def greet(j, carry):
        pl.semaphore_signal(barrier, inc=1, device_id={"dp": lax.rem(me + j, 32)}, device_id_type=MESH)
        return carry

    lax.fori_loop(1, 32, greet, 0)
    r = lax.broadcasted_iota(jnp.int32, (256, 256), 0)
    c = lax.broadcasted_iota(jnp.int32, (256, 256), 1)
    h_ref[...] = parity_signs(r, c).astype(jnp.bfloat16)
    r = lax.broadcasted_iota(jnp.int32, (128, 128), 0)
    c = lax.broadcasted_iota(jnp.int32, (128, 128), 1)
    w_ref[...] = jnp.where((r >> 6) == (c & 1), parity_signs(r & 63, c >> 1), 0.0).astype(jnp.bfloat16)
    seed_copy.wait()
    s0, s1, s2 = seed_ref[0], seed_ref[1], seed_ref[2] * 2048
    rows = lax.broadcasted_iota(jnp.int32, (8, 128), 0)
    cols = lax.broadcasted_iota(jnp.int32, (8, 128), 1)
    base = (rows * 128 + cols + feat * 4194304) * MULS[0] + s0
    upper = lax.shift_right_logical(rows, 1)
    lower = upper + 4

    def sign(n, qg, x_ref, s_ref):
        start = base + (n * 262144 + qg * 1024) * MULS[0]
        for u in range(2):
            vals = []
            for w4 in range(16):
                w = w4 * 2 + u
                v = start + wrap(w * 8192 * MULS[0])
                v = v ^ lax.shift_right_logical(v, 15)
                v = v * MULS[1] + s1
                v = v ^ lax.shift_right_logical(v, 13)
                v = v * wrap(MULS[2] * 2048) + s2
                flips = jnp.where(v < 0, -1.0, 1.0).astype(jnp.float32)
                pairs = [jnp.take_along_axis(flips, at, axis=0) for at in (upper, lower)]
                both = jnp.concatenate(pairs, axis=0).astype(jnp.bfloat16)
                vals.append(x_ref[w, pl.ds(aligned(qg * 16, 16), 16), :] * both)
            vals = butterflies(vals)
            for w4 in range(16):
                s_ref[w4, pl.ds(aligned(qg * 16, 16), 16), u * 128 : (u + 1) * 128] = vals[w4]

    def transform(n, pair, s_ref):
        rhs = s_ref[pl.ds(pair * 2, 2), :, :].reshape(256, 256)
        out = lax.dot_general(h_ref[...], rhs, NT_DIMS, preferred_element_type=jnp.float32)
        at = aligned(pair * 512, 512)
        t[n, pl.ds(at, 256), :] = out[:, :128]
        t[n, pl.ds(at + 256, 256), :] = out[:, 128:]

    def stage(n, s_write, s_read, signs=True):
        def body(i, carry):
            for a in range(UNROLL):
                if signs:
                    sign(n, i * UNROLL + a, xbuf.at[n & 3], s_write)
                if s_read is not None:
                    transform(n - 1, i * UNROLL + a, s_read)
            return carry

        lax.fori_loop(0, 8 // UNROLL, body, 0)

    def targets_to(j):
        return pltpu.make_async_remote_copy(
            src_ref=tgt.at[me],
            dst_ref=tgt.at[me],
            send_sem=send_sems.at[j],
            recv_sem=recv_sems.at[j],
            device_id={"dp": lax.rem(me + j, 32)},
            device_id_type=MESH,
        )

    def send_targets(j, carry):
        targets_to(j).start()
        return carry

    fetch(0).wait()
    for n in (2, 3):
        fetch(n).start()
    stage(0, sa, None)
    fetch(4).start()
    pl.semaphore_wait(barrier, 34)
    own_targets.wait()
    lax.fori_loop(1, 32, send_targets, 0)
    lane_copy.wait()
    low = lane_ref[...] & 4194303
    idx_v[...] = ((low >> 13) << 7) | (low & 127)

    def outer(j, carry):
        n = 2 * j + 1
        fetch(n).wait()
        stage(n, sb, sa)

        @pl.when(j < CHUNKS // 2 - 2)
        def _():
            fetch(n + 4).start()

        fetch(n + 1).wait()
        stage(n + 1, sa, sb)

        @pl.when(j < CHUNKS // 2 - 3)
        def _():
            fetch(n + 5).start()

        return carry

    lax.fori_loop(0, CHUNKS // 2 - 1, outer, 0)
    fetch(CHUNKS - 1).wait()
    stage(CHUNKS - 1, sb, sa)
    stage(CHUNKS, None, sb, signs=False)

    def indices(kb, idx_s, which):
        return pltpu.make_async_copy(idx_v.at[pl.ds(aligned(kb * 8, 8), 8), :], idx_s, idx_sems.at[which])

    indices(0, idx_a, 0).start()
    indices(1, idx_b, 1).start()

    def across(i, carry):
        for a in range(16):
            rows8 = pl.ds(aligned(i * 128, 128) + a * 8, 8)
            vals = butterflies([t[n, rows8, :] for n in range(CHUNKS)])
            for n in range(CHUNKS):
                t[n, rows8, :] = vals[n]
        return carry

    lax.fori_loop(0, 32, across, 0)
    flat = t.reshape(65536, 128)

    place = lax.broadcasted_iota(jnp.int32, (64, 128), 0)

    def finish(rows, quarter, at):
        out = lax.dot_general(
            w_ref[...], rows.astype(jnp.bfloat16), NT_DIMS, preferred_element_type=jnp.float32
        )
        for j in range(2):
            picked = lane_ref[pl.ds(quarter * 16 + at + j, 1), :]
            hit = place == ((picked >> 7) & 63)
            common = (picked >> 22) & feat
            scale = jnp.where((((common >> 1) ^ common) & 1) == 1, -1.0 / 4096, 1.0 / 4096)
            for e in range(2):
                mine = jnp.where(hit, out[e * 64 : (e + 1) * 64, j * 128 : (j + 1) * 128], 0.0)
                third = jnp.sum(mine, axis=0, keepdims=True)
                code[quarter, e, at + j : at + j + 1, :] = third * scale

    def pick(kb, which, g, before, quarter, at):
        idx_s = (idx_a, idx_b)[which]
        indices(kb, idx_s, which).wait()
        for j in range(8):
            if before is not None and j % 2 == 0:
                finish(before[j * 128 : (j + 2) * 128, :], quarter, at + j)
            for a in range(128):
                g[j * 128 + a : j * 128 + a + 1, :] = flat[pl.ds(idx_s[j, a], 1), :]

    pick(0, 0, ga, None, 0, 0)
    indices(2, idx_a, 0).start()

    def pick_two(i, carry):
        kb = 2 * i + 1
        pick(kb, 1, gb, ga, i, 0)
        indices(kb + 2, idx_b, 1).start()
        pick(kb + 1, 0, ga, gb, i, 8)

        @pl.when(i < 2)
        def _():
            indices(kb + 3, idx_a, 0).start()

        return carry

    lax.fori_loop(0, 3, pick_two, 0)
    pick(7, 1, gb, ga, 3, 0)
    for j in range(0, 8, 2):
        finish(gb[j * 128 : (j + 2) * 128, :], 3, 8 + j)
    term[...] = code[...].astype(jnp.bfloat16)

    def to_peer(source, landing, slot, d):
        return pltpu.make_async_remote_copy(
            src_ref=source,
            dst_ref=landing,
            send_sem=feat_sems.at[slot, 0, d],
            recv_sem=feat_sems.at[slot, 1, d],
            device_id={"feat": peers[d]},
            device_id_type=MESH,
        )

    terms = [to_peer(term.at[peers[d]], got.at[d], 0, d) for d in range(3)]
    for copy in terms:
        copy.start()
    def wait_targets(j, carry):
        targets_to(j).wait()
        return carry

    lax.fori_loop(1, 32, wait_targets, 0)
    squares = []
    for b in range(4):
        total = jnp.zeros((128, 128), jnp.float32)
        for r in range(16):
            wide = tgt[b * 8 : (b + 1) * 8, :, r * 128 : (r + 1) * 128].reshape(128, 128).astype(jnp.float32)
            total = total + wide * wide
        squares.append(total)
    squares = jnp.concatenate(squares, axis=0)
    ones = jnp.ones((8, 128), jnp.float32)
    target_squares = lax.dot_general(
        ones, squares, NT_DIMS, precision=lax.Precision.HIGHEST, preferred_element_type=jnp.float32
    )
    for copy in terms:
        copy.wait()
    own = term[feat].astype(jnp.float32)
    for d in range(3):
        own = own + got[d].astype(jnp.float32)
    sketch = own.astype(jnp.bfloat16).astype(jnp.float32)
    lhs[...] = jnp.zeros_like(lhs)
    for e in range(2):
        for r in range(16):
            lhs[e : e + 1, r * 128 : (r + 1) * 128] = sketch[e, r : r + 1, :]
    wide = lhs[...]
    own_squares = jnp.sum(wide * wide, axis=1, keepdims=True)
    dots = lax.dot_general(
        wide.astype(jnp.bfloat16), tgt[...].reshape(512, 2048), NT_DIMS, preferred_element_type=jnp.float32
    )
    part[feat, 0] = dots
    part[feat, 1] = target_squares
    part[feat, 2] = jnp.broadcast_to(own_squares, (8, 512))
    parts = [to_peer(part.at[feat], part.at[feat], 1, d) for d in range(3)]
    for copy in parts:
        copy.start()
    group_copy.wait()
    member = (lax.broadcasted_iota(jnp.int32, (128, 512), 0) == group_ref[...]).astype(jnp.float32)
    member = member.astype(jnp.bfloat16)
    for copy in parts:
        copy.wait()
    whole = (part[0] + part[1]) + (part[2] + part[3])
    scores = whole[0] * lax.rsqrt(whole[2] + EPS) * lax.rsqrt(whole[1] + EPS) * math.sqrt(8192)
    at = lax.broadcasted_iota(jnp.int32, (8, 512), 0)
    rest = scores
    sums = jnp.zeros((8, 128), jnp.float32)
    for piece in range(3):
        top = rest.astype(jnp.bfloat16)
        rest = rest - top.astype(jnp.float32)
        filled = jnp.where(at < 2, top.astype(jnp.float32), 1.0 if piece == 0 else 0.0)
        sums = sums + lax.dot_general(
            filled.astype(jnp.bfloat16), member, NT_DIMS, preferred_element_type=jnp.float32
        )
    scores_ref[...] = scores[:2]
    means_ref[...] = sums[:2, :TASKS] / sums[2:3, :TASKS]


def shards(gradients, sign_seed, sample_index, target_sketches, target_group):
    x = gradients.reshape(2, 32768, 128).transpose(1, 0, 2).reshape(512, 128, 128)
    vmem = pltpu.VMEM
    whole = pl.BlockSpec(memory_space=pltpu.VMEM)
    dma = pltpu.SemaphoreType.DMA
    return pl.pallas_call(
        whole_kernel,
        out_shape=(
            jax.ShapeDtypeStruct((2, 512), jnp.float32),
            jax.ShapeDtypeStruct((2, TASKS), jnp.float32),
        ),
        in_specs=[pl.BlockSpec(memory_space=pltpu.HBM)] * 5,
        out_specs=(whole, whole),
        scratch_shapes=[
            vmem((4, 32, 128, 128), jnp.bfloat16),
            vmem((16, 128, 256), jnp.bfloat16),
            vmem((16, 128, 256), jnp.bfloat16),
            vmem((16, 4096, 128), jnp.float32),
            vmem((1024, 128), jnp.float32),
            vmem((1024, 128), jnp.float32),
            vmem((256, 256), jnp.bfloat16),
            vmem((128, 128), jnp.bfloat16),
            vmem((4, 2, 16, 128), jnp.float32),
            pltpu.SMEM((3,), jnp.int32),
            vmem((64, 128), jnp.int32),
            vmem((1, 512), jnp.int32),
            vmem((64, 128), jnp.int32),
            pltpu.SMEM((8, 128), jnp.int32),
            pltpu.SMEM((8, 128), jnp.int32),
            vmem((4, 2, 16, 128), jnp.bfloat16),
            vmem((3, 2, 16, 128), jnp.bfloat16),
            vmem((8, 2048), jnp.float32),
            vmem((32, 16, 2048), jnp.bfloat16),
            vmem((4, 3, 8, 512), jnp.float32),
            dma((4,)),
            dma((4,)),
            dma((2,)),
            dma((32,)),
            dma((32,)),
            dma((2, 2, 3)),
        ],
        compiler_params=pltpu.CompilerParams(
            collective_id=0, has_side_effects=True, vmem_limit_bytes=58 * 1024 * 1024
        ),
    )(sign_seed, sample_index.reshape(64, 128), target_group.reshape(1, 512), target_sketches, x)


def solution(mesh):
    in_specs = (P("dp", "feat"), P(), P(), P("dp", None), P())
    out_specs = (P("dp", None), P("dp", None))
    return jax.shard_map(shards, mesh=mesh, in_specs=in_specs, out_specs=out_specs, check_vma=False)
```
